128 devices in a mesh: grp: 16 (over x_lo, y, core), hd: 8 (over x_hi, z).
Axes of the slice: x: 4 (x_hi: 2, x_lo: 2; x = x_hi * 2 + x_lo), y: 4, z: 4, core: 2. Of those that a mesh axis runs over, the one named last changes fastest.
Arguments:
- query_rows: bfloat16 [16, 1024, 8192], P('grp', 'hd'), may hold values from -8 to 8
- key_rows: bfloat16 [16, 1024, 1024], P('grp', 'hd'), may hold values from -8 to 8
- value_rows: bfloat16 [16, 1024, 1024], P('grp', 'hd'), may hold values from -6 to 6
- lengths: int32 [16], replicated, may hold values from 256 to 1024, as said below
Outputs:
- attended: bfloat16 [16, 1024, 8192], P('grp', 'hd')
The draws below stay inside these ranges and needn't reach their ends.
Inputs may be any that keep to these rules, and one draw needn't show every extreme that they name: `lengths`: each length lies in 256 to 1024; some sequence has length exactly 1024.
All inputs are finite; a program needn't handle non-finite values.
Results may differ from the reference program's by a relative error of at most 0.0044.
Values may be sent and summed in bfloat16 or wider, within the bound.
No kernel may reach another device: no remote copies, remote signals or barrier semaphores. Data moves between devices by JAX's collectives and lax.ppermute only.
A program may use at most 128 MiB of HBM per device.

```python
import math
import jax
import jax.numpy as jnp
from jax import lax

H = 64
KVH = 8
DH = 128
S = 1024
NGROUPS = 16


def draw_query_rows(key, part):
    key = jax.random.fold_in(key, 5)
    shape = (NGROUPS, S, H * DH)
    base = jnp.clip(jax.random.normal(key, shape, jnp.float32), -4.0, 4.0)
    return base.astype(jnp.bfloat16)


def draw_key_rows(key, part):
    key = jax.random.fold_in(key, 6)
    shape = (NGROUPS, S, KVH * DH)
    base = jnp.clip(jax.random.normal(key, shape, jnp.float32), -4.0, 4.0)
    return base.astype(jnp.bfloat16)


def draw_lengths(key, part):
    key = jax.random.fold_in(key, 1)
    drawn = jax.random.randint(key, (NGROUPS,), S // 4, S + 1)
    longest = jax.random.randint(jax.random.fold_in(key, 2), (), 0, NGROUPS)
    return jnp.where(jnp.arange(NGROUPS) == longest, S, drawn).astype(jnp.int32)


def steps_of(rng, dims, pieces, low, top_value):
    def one(position, shards_of):
        draws = jax.random.uniform(jax.random.fold_in(jax.random.fold_in(rng, 6), position), (shards_of,), jnp.float32, low / len(pieces), top_value / len(pieces))
        return jnp.repeat(jnp.exp(draws), dims[position] // shards_of).reshape((-1,) + (1,) * (len(dims) - position - 1))

    level = one(*pieces[0])
    for cut in pieces[1:]:
        level = level * one(*cut)
    return level


def scatter_about(key, extent, deviation, limit, shards=(), kind=jnp.bfloat16):
    entries = jax.random.normal(key, extent, jnp.float32) * deviation
    if len(shards) > 0:
        entries = steps_of(key, extent, shards, -0.22, 0.18) * entries
    return jnp.clip(entries, min=-limit, max=limit).astype(kind)


def setup_inputs(seed: int = 0) -> dict:
    splits = jax.random.split(jax.random.key(seed), 5)
    query_rows = draw_query_rows(jax.random.fold_in(splits[4], 71), 0)
    key_rows = draw_key_rows(jax.random.fold_in(splits[4], 71), 0)
    value_rows = scatter_about(splits[2], (NGROUPS, S, KVH * DH), 1.0, 6.0, ((0, 16), (1, 8)))
    lengths = draw_lengths(jax.random.fold_in(splits[4], 71), 0)
    return {"query_rows": query_rows, "key_rows": key_rows, "value_rows": value_rows, "lengths": lengths}


def attend(own_q, query_pos, own_k, own_v, pre_k, pre_v, own_len, pre_len, is_prompt):
    row_count = own_q.shape[0]
    key_span = own_k.shape[0]
    kv_count = own_k.shape[1] // DH
    group_size = own_q.shape[1] // DH // kv_count
    all_keys = jnp.concatenate([pre_k, own_k], 0).reshape(2 * key_span, kv_count, DH).transpose(1, 0, 2)
    all_values = jnp.concatenate([pre_v, own_v], 0).reshape(2 * key_span, kv_count, DH).transpose(1, 0, 2)
    heads_q = own_q.reshape(row_count, kv_count, group_size, DH).transpose(1, 0, 2, 3)
    key_pos = jnp.arange(key_span, dtype=jnp.int32)
    pre_ok = (key_pos < pre_len) & jnp.logical_not(is_prompt)
    own_ok = (key_pos[None, :] <= query_pos[:, None]) & (key_pos[None, :] < own_len)
    allowed = jnp.concatenate([jnp.broadcast_to(pre_ok[None, :], (row_count, key_span)), own_ok], 1)
    score_scale = 1.0 / math.sqrt(DH)

    def per_head(triple):
        q_head, k_head, v_head = triple
        scores = jnp.einsum('qgd,kd->gqk', q_head.astype(jnp.float32), k_head.astype(jnp.float32)) * score_scale
        scores = jnp.where(allowed[None], scores, jnp.float32(-1e+30))
        row_top = lax.optimization_barrier(jnp.max(scores, -1, keepdims=True))
        probs = jnp.exp(scores - row_top)
        total = lax.optimization_barrier(jnp.sum(probs, -1))
        weights = probs.astype(jnp.bfloat16)
        mixed = jnp.einsum('gqk,kd->gqd', weights.astype(jnp.float32), v_head.astype(jnp.float32))
        return (mixed / total[..., None]).transpose(1, 0, 2)
    result = lax.map(per_head, (heads_q, all_keys, all_values))
    result = result.transpose(1, 0, 2, 3).reshape(row_count, -1)
    live = query_pos < own_len
    return jnp.where(live[:, None], result, 0.0).astype(jnp.bfloat16)

def reference(query_rows, key_rows, value_rows, lengths):
    prompt_len = lengths[0]
    positions = jnp.arange(S, dtype=jnp.int32)

    def per_group(index):
        return attend(query_rows[index], positions, key_rows[index], value_rows[index], key_rows[0], value_rows[0], lengths[index], prompt_len, index == 0)
    return lax.map(per_group, jnp.arange(NGROUPS, dtype=jnp.int32))
```

```python
import functools
import math

import jax
import jax.numpy as jnp
from jax import lax
from jax.experimental import pallas as pl
from jax.experimental.pallas import tpu as pltpu
from jax.sharding import PartitionSpec as P

DH = 128
ROWS = 128
KVH = 8
GROUP = 8
PAIR = 2 * DH
SCALE_LOG2 = math.log2(math.e) / math.sqrt(DH)
NEG = -1e30
NT = (((1,), (1,)), ((), ()))
TILE = 512


def attend_kernel(
    info, q_ref, diag, r0p, r0m, r1m, r0x, r1x, r1p, r2a, r2b, *rest
):
    prompt, (o_ref, k_aug, v_aug) = rest[:KVH], rest[KVH:]
    step = pl.program_id(0)
    head = info[step]
    x_hi, z, pre_len, n_live = info[8], info[9], info[10], info[11]
    lane0 = lax.broadcasted_iota(jnp.int32, (ROWS, DH), 1) == 0
    neg = jnp.float32(NEG)

    def place(slot, ref, bias):
        rows = slice(slot * ROWS, (slot + 1) * ROWS)
        k_aug[rows, :DH] = ref[:, :DH]
        v_aug[rows, :DH] = ref[:, DH:]
        k_aug[rows, DH:] = jnp.where(lane0, bias, 0.0).astype(jnp.bfloat16)

    @pl.when(step == 0)
    def _():
        v_aug[:, DH:] = jnp.ones((2048, DH), jnp.bfloat16)

    def bias_if(ok):
        return jnp.where(ok, jnp.float32(0.0), neg)

    place(0, diag, jnp.float32(0.0))
    place(1, r0p, bias_if(z >= 1))
    place(2, r0m, bias_if(z == 3))
    place(3, r1m, bias_if(z >= 2))
    place(4, r0x, bias_if(x_hi == 1))
    place(5, r1x, bias_if(x_hi == 1))
    place(6, r1p, bias_if(x_hi == 1))

    @pl.when(head < 4)
    def _():
        place(7, r2a, bias_if(x_hi == 1))

    @pl.when(head >= 4)
    def _():
        place(7, r2b, bias_if(x_hi == 1))

    for n in range(KVH):

        @pl.when(step == n)
        def _(n=n):
            k_aug[1024:, :DH] = prompt[n][:, :DH]
            v_aug[1024:, :DH] = prompt[n][:, DH:]

    position = lax.broadcasted_iota(jnp.int32, (1024, DH), 0)
    first = lax.broadcasted_iota(jnp.int32, (1024, DH), 1) == 0
    k_aug[1024:, DH:] = jnp.where(first & (position >= pre_len), neg, 0.0).astype(jnp.bfloat16)

    chunks = (pre_len + 255) // 256

    def run(n_keys):
        heads_in_tile = TILE // ROWS
        row = lax.broadcasted_iota(jnp.int32, (TILE, ROWS), 0) % ROWS
        col = lax.broadcasted_iota(jnp.int32, (TILE, ROWS), 1)
        one = jnp.where(
            lax.broadcasted_iota(jnp.int32, (TILE, DH), 1) == 0, 1.0, 0.0
        ).astype(jnp.bfloat16)
        for t in range(GROUP * ROWS // TILE):
            q = jnp.concatenate(
                [
                    q_ref[:, (t * heads_in_tile + j) * DH : (t * heads_in_tile + j + 1) * DH]
                    for j in range(heads_in_tile)
                ],
                0,
            )
            q = jnp.concatenate([q, one], 1)
            s = lax.dot_general(q, k_aug[:n_keys, :], NT, preferred_element_type=jnp.float32)
            s = jnp.concatenate([jnp.where(row >= col, s[:, :ROWS], neg), s[:, ROWS:]], 1)
            top = jnp.max(s, axis=1, keepdims=True)
            p = jnp.exp2((s - top) * SCALE_LOG2).astype(jnp.bfloat16)
            acc = jnp.dot(p, v_aug[:n_keys, :], preferred_element_type=jnp.float32)
            out = acc[:, :DH] / acc[:, DH:]
            out = jnp.where(row < n_live, out, 0.0).astype(jnp.bfloat16)
            for j in range(heads_in_tile):
                h = t * heads_in_tile + j
                o_ref[:, h * DH : (h + 1) * DH] = out[j * ROWS : (j + 1) * ROWS]

    for n in range(5):

        @pl.when((n_live > 0) & (chunks == n))
        def _(n=n):
            run(1024 + 256 * n)

    @pl.when(n_live <= 0)
    def _():
        o_ref[...] = jnp.zeros_like(o_ref)


def attend(info, query, own, prompt):
    def at_head(width):
        return pl.BlockSpec((ROWS, width), lambda i, info: (0, info[i]))

    half = pl.BlockSpec((ROWS, PAIR), lambda i, info: (0, lax.rem(info[i], 4)))
    whole = pl.BlockSpec((1024, PAIR), lambda i, info: (0, 0))
    return pl.pallas_call(
        attend_kernel,
        grid_spec=pltpu.PrefetchScalarGridSpec(
            num_scalar_prefetch=1,
            grid=(KVH,),
            in_specs=[at_head(GROUP * DH)] + [at_head(PAIR)] * 7 + [half] * 2 + [whole] * KVH,
            out_specs=at_head(GROUP * DH),
            scratch_shapes=[
                pltpu.VMEM((2048, PAIR), jnp.bfloat16),
                pltpu.VMEM((2048, PAIR), jnp.bfloat16),
            ],
        ),
        out_shape=jax.ShapeDtypeStruct(query.shape, jnp.bfloat16),
        compiler_params=pltpu.CompilerParams(vmem_limit_bytes=48 << 20),
    )(info, query, *own, *prompt)


def on_device(query_rows, key_rows, value_rows, lengths):
    grp = lax.axis_index("grp")
    hd = lax.axis_index("hd")
    core, y, x_lo = grp % 2, (grp // 2) % 4, grp // 8
    z, x_hi = hd % 4, hd // 4

    kv = jnp.concatenate(
        [key_rows[0].reshape(ROWS, KVH, DH), value_rows[0].reshape(ROWS, KVH, DH)], 2
    ).reshape(ROWS, KVH * PAIR)

    def on_hd(value, pairs):
        return lax.ppermute(value, "hd", pairs)

    def on_grp(value, pairs):
        return lax.ppermute(value, "grp", pairs)

    other = on_grp(kv[:, 4 * PAIR :], [(0, 1)])
    four = jnp.where(core == 0, kv[:, : 4 * PAIR], other)
    piece = four[:, :PAIR]
    for d in range(1, 4):
        got = on_grp(four[:, d * PAIR : (d + 1) * PAIR], [(0, 2 * d), (1, 2 * d + 1)])
        piece = jnp.where(y == d, got, piece)

    r0x = on_hd(kv, [(i, 4 + i) for i in range(4)])
    r0p = on_hd(kv, [(4 * x + i, 4 * x + i + 1) for x in range(2) for i in range(3)])
    r0m = on_hd(kv, [((i + 1) % 4, i) for i in range(4)] + [(4, 7), (5, 4)])

    def on_both(value, pairs):
        return lax.ppermute(value, ("grp", "hd"), pairs)

    c1 = on_both(piece, [(g * 8 + r, (g + 8) * 8 + r) for g in range(8) for r in range(8)])
    c2 = on_both(piece, [(g * 8 + r, g * 8 + (r ^ 4)) for g in range(8) for r in range(8)])
    c3 = on_both(piece, [(g * 8 + r, (g + 8) * 8 + (r ^ 4)) for g in range(8) for r in range(8)])
    same = jnp.where(x_lo == 0, piece, c1)
    far = jnp.where(x_lo == 0, c2, c3)
    both = jnp.stack([jnp.where(x_hi == 0, same, far), jnp.where(x_hi == 0, far, same)])

    def ring(d):
        return [(4 * x + i, 4 * x + (i + d) % 4) for x in range(2) for i in range(4)]

    behind = [both] + [on_hd(both, ring(d)) for d in range(1, 4)]
    orders = [
        jnp.stack([behind[(at - i) % 4] for i in range(4)], 1).reshape(1024, PAIR)
        for at in range(4)
    ]
    mine = lax.select_n(z, *orders)

    r1x = on_hd(r0m, [(i, 4 + i) for i in range(4)])
    r1p = on_hd(r0x, [(4 + i, 4 + (i + 1) % 4) for i in range(4)])
    r1m = on_hd(r0m, [((i + 1) % 4, i) for i in range(4)] + [(7, 6), (4, 7)])
    r2a = on_hd(r1m[:, : 4 * PAIR], [(i, 4 + i) for i in range(4)])
    r2b = on_hd(r1p[:, 4 * PAIR :], [(4 + i, 4 + (i + 1) % 4) for i in range(4)])

    def along_y(d):
        return [(g, (g & 9) | ((g + 2 * d) & 6)) for g in range(16)]

    fours = [mine] + [on_grp(mine, along_y(d)) for d in range(1, 4)]
    swapped = [on_grp(value, [(g, g ^ 1) for g in range(16)]) for value in fours]
    heads = [4 * core + (y - d) % 4 for d in range(4)]
    heads += [4 * (1 - core) + (y - d) % 4 for d in range(4)]

    pre_len = jnp.where(grp == 0, 0, lengths[0])
    n_live = lengths[grp] - hd * ROWS
    info = jnp.stack([jnp.int32(v) for v in heads + [x_hi, z, pre_len, n_live]])
    own = (kv, r0p, r0m, r1m, r0x, r1x, r1p, r2a, r2b)
    return attend(info, query_rows[0], own, fours + swapped)[None]


def solution(mesh):
    placed = (P("grp", "hd", None), P("grp", "hd", None), P("grp", "hd", None), P())
    return jax.shard_map(
        on_device, mesh=mesh, in_specs=placed, out_specs=P("grp", "hd", None), check_vma=False
    )
```

```python
import math

import jax
import jax.numpy as jnp
from jax import lax
from jax.experimental import pallas as pl
from jax.experimental.pallas import tpu as pltpu
from jax.sharding import PartitionSpec as P

DH = 128
ROWS = 128
KVH = 8
GROUP = 8
PAIR = 2 * DH
SCALE_LOG2 = math.log2(math.e) / math.sqrt(DH)
NEG = -1e30
LEAST, MOST = 2.0**-80, 2.0**100
NT = (((1,), (1,)), ((), ()))
TILE = 256
IN_TILE = TILE // ROWS
PARAMS = pltpu.CompilerParams(vmem_limit_bytes=24 << 20)


def cost(heads, keys):
    pairs = GROUP * heads * ROWS * keys
    return pl.CostEstimate(flops=8 * pairs * DH, bytes_accessed=1 << 22, transcendentals=pairs)


def tiles(q_ref, head):
    for t in range(GROUP // IN_TILE):
        lanes = [lane_of(head, h) for h in range(t * IN_TILE, (t + 1) * IN_TILE)]
        yield t, jnp.concatenate([q_ref[:, lane] for lane in lanes], 0)


def lane_of(head, h):
    return pl.ds(pl.multiple_of((head * GROUP + h) * DH, DH), DH)


def causal_mask():
    row = lax.broadcasted_iota(jnp.int32, (TILE, ROWS), 0) % ROWS
    return row >= lax.broadcasted_iota(jnp.int32, (TILE, ROWS), 1)


def sweep(q_ref, head, k_scr, v_scr, n_keys, causal, put):
    for t, q in tiles(q_ref, head):
        s = lax.dot_general(q, k_scr[:n_keys, :], NT, preferred_element_type=jnp.float32)
        s = s * SCALE_LOG2
        if causal:
            s = jnp.concatenate([jnp.where(causal_mask(), s[:, :ROWS], NEG), s[:, ROWS:]], 1)
        p = jnp.exp2(s).astype(jnp.bfloat16)
        sums = jnp.dot(p, v_scr[:n_keys, :], preferred_element_type=jnp.float32)
        for j in range(IN_TILE):
            put(t * IN_TILE + j, sums[j * ROWS : (j + 1) * ROWS])


def place(k_scr, v_scr, slot, ref, ok):
    rows = slice(slot * ROWS, (slot + 1) * ROWS)
    k_scr[rows, :] = ref[:, :DH]
    v_scr[rows, :DH] = jnp.where(ok, ref[:, DH:], jnp.zeros_like(ref[:, DH:]))
    v_scr[rows, DH:] = jnp.where(ok, jnp.ones((ROWS, DH), jnp.float32), 0.0).astype(jnp.bfloat16)


def own_blocks(info):
    z, right = info[9], info[8] == 1
    return (True, z >= 1, z == 3, z >= 2, right, right, right, right)


def own_kernel(info, q_ref, *rest):
    blocks, (tot_ref, acc_ref, k_own, v_own) = rest[:9], rest[9:]
    head = pl.program_id(0)
    allowed = own_blocks(info)
    columns = pl.ds(pl.multiple_of(head * PAIR, PAIR), PAIR)
    half = pl.ds(pl.multiple_of(lax.rem(head, 4) * PAIR, PAIR), PAIR)

    @pl.when(info[11] > 0)
    def _():
        for slot in range(4):
            place(k_own, v_own, slot, blocks[slot][:, columns], allowed[slot])

        for slot in range(4, 7):
            place(k_own, v_own, slot, blocks[slot][:, columns], allowed[slot])

        @pl.when(head < 4)
        def _():
            place(k_own, v_own, 7, blocks[7][:, half], allowed[7])

        @pl.when(head >= 4)
        def _():
            place(k_own, v_own, 7, blocks[8][:, half], allowed[7])

        lane = lax.broadcasted_iota(jnp.int32, (ROWS, DH), 1)
        totals = []

        def put(h, sums):
            acc_ref[:, lane_of(head, h)] = sums[:, :DH]
            totals.append(jnp.where(lane == h, sums[:, DH:], totals[-1] if totals else 0.0))

        sweep(q_ref, head, k_own, v_own, 8 * ROWS, True, put)
        tot_ref[:, pl.ds(pl.multiple_of(head * DH, DH), DH)] = totals[-1]


def prompt_kernel(info, q_ref, tot_in, acc_in, *rest):
    prompt, stored, rest = rest[:KVH], rest[KVH : KVH + 9], rest[KVH + 9 :]
    o_ref, k_pre, v_pre, flag = rest[:4]
    step = pl.program_id(0)
    head = info[step]
    pre_len, n_live = info[10], info[11]
    chunks = (pre_len + 255) // 256
    row = lax.broadcasted_iota(jnp.int32, (ROWS, DH), 0)

    @pl.when(step == 0)
    def _():
        live = lax.broadcasted_iota(jnp.int32, (8 * ROWS, DH), 0) < pre_len
        v_pre[:, DH:] = jnp.where(live, 1.0, 0.0).astype(jnp.bfloat16)

    @pl.when(n_live > 0)
    def _():
        for n, buffer in enumerate(prompt):

            @pl.when(step == n)
            def _(buffer=buffer):
                k_pre[...] = buffer[:, :DH]
                v_pre[:, :DH] = buffer[:, DH:]

        flag[...] = jnp.zeros_like(flag)

        def finish(h, sums):
            totals = tot_in[:, pl.ds(pl.multiple_of(head * DH, DH), DH)]
            total = totals[:, h : h + 1]
            out = acc_in[:, lane_of(head, h)]
            if sums is None:
                total = jnp.broadcast_to(total, (ROWS, DH))
            else:
                total = total + sums[:, DH:]
                out = out + sums[:, :DH]
            wrong = jnp.where((total >= LEAST) & (total <= MOST), 0.0, 1.0)
            flag[...] = jnp.maximum(flag[...], jnp.where(row < n_live, wrong, 0.0))
            out = jnp.where(row < n_live, out / total, 0.0)
            o_ref[:, h * DH : (h + 1) * DH] = out.astype(jnp.bfloat16)

        @pl.when(chunks == 0)
        def _():
            for h in range(GROUP):
                finish(h, None)

        for n in range(1, 5):

            @pl.when(chunks == n)
            def _(n=n):
                sweep(q_ref, head, k_pre, v_pre, 256 * n, False, finish)

        @pl.when(jnp.max(flag[...]) > 0.5)
        def _():
            with_largest(info, head, q_ref, k_pre, v_pre, stored, o_ref, *rest[4:])

    @pl.when(n_live <= 0)
    def _():
        o_ref[...] = jnp.zeros_like(o_ref)


def with_largest(info, head, q_ref, k_pre, v_pre, stored, o_ref, k_aug, v_aug, land, sem):
    pre_len, n_live = info[10], info[11]
    allowed = own_blocks(info)

    def put(rows, count, key, value, ok):
        first = lax.broadcasted_iota(jnp.int32, (count, DH), 1) == 0
        k_aug[rows, :DH] = key
        k_aug[rows, DH:] = jnp.where(first & jnp.logical_not(ok), NEG, 0.0).astype(jnp.bfloat16)
        v_aug[rows, :DH] = value
        v_aug[rows, DH:] = jnp.ones((count, DH), jnp.bfloat16)

    def fetch(source, columns):
        copy = pltpu.make_async_copy(source.at[:, columns], land, sem)
        copy.start()
        copy.wait()

    columns = pl.ds(pl.multiple_of(head * PAIR, PAIR), PAIR)
    half = pl.ds(pl.multiple_of(lax.rem(head, 4) * PAIR, PAIR), PAIR)
    for slot in range(8):
        if slot < 7:
            fetch(stored[slot], columns)
        else:
            for low, source in ((True, stored[7]), (False, stored[8])):

                @pl.when((head < 4) == low)
                def _(source=source):
                    fetch(source, half)

        rows = slice(slot * ROWS, (slot + 1) * ROWS)
        put(rows, ROWS, land[:, :DH], land[:, DH:], allowed[slot])
    position = lax.broadcasted_iota(jnp.int32, (8 * ROWS, DH), 0)
    rows = slice(8 * ROWS, 16 * ROWS)
    put(rows, 8 * ROWS, k_pre[...], v_pre[:, :DH], position < pre_len)

    row = lax.broadcasted_iota(jnp.int32, (ROWS, PAIR), 0)
    col = lax.broadcasted_iota(jnp.int32, (ROWS, PAIR), 1)
    one = jnp.where(col[:, :DH] == 0, 1.0, 0.0).astype(jnp.bfloat16)

    @pl.loop(0, GROUP)
    def _(h):
        lane = pl.ds(pl.multiple_of(h * DH, DH), DH)
        q = jnp.concatenate([q_ref[:, lane_of(head, h)], one], 1)

        def scores(c):
            keys = pl.ds(pl.multiple_of(c * PAIR, PAIR), PAIR)
            s = lax.dot_general(q, k_aug[keys, :], NT, preferred_element_type=jnp.float32)
            return jnp.where((row >= col) | (col >= ROWS) | (c > 0), s, NEG), keys

        def largest(c, top):
            return jnp.maximum(top, jnp.max(scores(c)[0], axis=1, keepdims=True))

        top = lax.fori_loop(0, 8, largest, jnp.full((ROWS, 1), NEG, jnp.float32))

        def weigh(c, acc):
            s, keys = scores(c)
            p = jnp.exp2((s - top) * SCALE_LOG2).astype(jnp.bfloat16)
            return acc + jnp.dot(p, v_aug[keys, :], preferred_element_type=jnp.float32)

        acc = lax.fori_loop(0, 8, weigh, jnp.zeros((ROWS, PAIR), jnp.float32))
        out = jnp.where(row[:, :DH] < n_live, acc[:, :DH] / acc[:, DH:], 0.0)
        o_ref[:, lane] = out.astype(jnp.bfloat16)


VMEM = pl.BlockSpec(memory_space=pltpu.VMEM)
ANY = pl.BlockSpec(memory_space=pl.ANY)


def scratch():
    return [
        pltpu.VMEM((8 * ROWS, DH), jnp.bfloat16),
        pltpu.VMEM((8 * ROWS, PAIR), jnp.bfloat16),
    ]


def attend_own(info, query, own):
    return pl.pallas_call(
        own_kernel,
        grid_spec=pltpu.PrefetchScalarGridSpec(
            num_scalar_prefetch=1,
            grid=(KVH,),
            in_specs=[VMEM] * (1 + len(own)),
            out_specs=(VMEM, VMEM),
            scratch_shapes=scratch(),
        ),
        out_shape=(
            jax.ShapeDtypeStruct((ROWS, KVH * DH), jnp.float32),
            jax.ShapeDtypeStruct((ROWS, KVH * GROUP * DH), jnp.float32),
        ),
        compiler_params=PARAMS,
        cost_estimate=cost(KVH, 8 * ROWS),
        name="own",
    )(info, query, *own)


def attend_prompt(info, query, state, prompt, own):
    return pl.pallas_call(
        prompt_kernel,
        grid_spec=pltpu.PrefetchScalarGridSpec(
            num_scalar_prefetch=1,
            grid=(KVH,),
            in_specs=[VMEM] * (3 + len(prompt)) + [ANY] * len(own),
            out_specs=pl.BlockSpec((ROWS, GROUP * DH), lambda i, info: (0, info[i])),
            scratch_shapes=scratch()
            + [
                pltpu.VMEM((ROWS, DH), jnp.float32),
                pltpu.VMEM((16 * ROWS, PAIR), jnp.bfloat16),
                pltpu.VMEM((16 * ROWS, PAIR), jnp.bfloat16),
                pltpu.VMEM((ROWS, PAIR), jnp.bfloat16),
                pltpu.SemaphoreType.DMA(()),
            ],
        ),
        out_shape=jax.ShapeDtypeStruct(query.shape, jnp.bfloat16),
        compiler_params=PARAMS,
        cost_estimate=cost(KVH, 8 * ROWS),
        name="prompt",
    )(info, query, *state, *prompt, *own)


def pair_kernel(k_ref, v_ref, o_ref, top_ref):
    for h in range(KVH):
        o_ref[:, h * PAIR : h * PAIR + DH] = k_ref[:, h * DH : (h + 1) * DH]
        o_ref[:, h * PAIR + DH : (h + 1) * PAIR] = v_ref[:, h * DH : (h + 1) * DH]
    top_ref[...] = o_ref[:, 4 * PAIR :]


def pair_up(keys, values):
    return pl.pallas_call(
        pair_kernel,
        out_shape=(
            jax.ShapeDtypeStruct((ROWS, KVH * PAIR), jnp.bfloat16),
            jax.ShapeDtypeStruct((ROWS, 4 * PAIR), jnp.bfloat16),
        ),
    )(keys, values)


def on_device(query_rows, key_rows, value_rows, lengths):
    grp = lax.axis_index("grp")
    hd = lax.axis_index("hd")
    core, y, x_lo = grp % 2, (grp // 2) % 4, grp // 8
    z, x_hi = hd % 4, hd // 4
    query = query_rows[0]
    kv, top = pair_up(key_rows[0], value_rows[0])

    def on_hd(value, pairs):
        return lax.ppermute(value, "hd", pairs)

    def on_grp(value, pairs):
        return lax.ppermute(value, "grp", pairs)

    def along_y(value, d):
        return on_grp(value, [(g, (g & 9) | ((g + 2 * d) & 6)) for g in range(16)])

    def along_z(value, d):
        return on_hd(value, [(4 * x + i, 4 * x + (i + d) % 4) for x in range(2) for i in range(4)])

    def swap(value):
        return on_grp(value, [(g, g ^ 1) for g in range(16)])

    def along_x_hi(value):
        return on_hd(value, [(i, i ^ 4) for i in range(8)])

    tie = lax.optimization_barrier

    steps = (0, 1, 3, 2)
    heads = [4 * c + (y - d) % 4 for d in steps for c in (core, 1 - core)]
    pre_len = jnp.where(grp == 0, 0, lengths[0])
    n_live = lengths[grp] - hd * ROWS
    info = jnp.stack([jnp.int32(v) for v in heads + [x_hi, z, pre_len, n_live]])

    r0x, r0p, r0m = along_x_hi(kv), along_z(kv, 1), along_z(kv, 3)
    four = jnp.where(core == 0, kv[:, : 4 * PAIR], swap(top))
    two = jnp.where(y == 2, along_y(four[:, 2 * PAIR :], 2), four[:, : 2 * PAIR])
    r0x, r0p, r0m, two = tie((r0x, r0p, r0m, two))

    r1x, r1p, r1m = along_x_hi(r0m), along_z(r0x, 1), along_z(r0m, 3)
    one = jnp.where(y % 2 == 1, along_y(two[:, PAIR:], 1), two[:, :PAIR])
    r1x, r1p, r1m, one = tie((r1x, r1p, r1m, one))

    r2a, r2b = along_x_hi(r1m[:, : 4 * PAIR]), along_z(r1p[:, 4 * PAIR :], 1)
    piece = jnp.where(x_lo == 0, one, on_grp(one, [(g, g ^ 8) for g in range(16)]))
    other = along_x_hi(piece)
    both = jnp.stack(
        [jnp.where(x_hi == 0, piece, other), jnp.where(x_hi == 0, other, piece)]
    )
    behind = [both] + [along_z(both, d) for d in range(1, 4)]
    orders = [
        jnp.stack([behind[(at - i) % 4] for i in range(4)], 1).reshape(8 * ROWS, PAIR)
        for at in range(4)
    ]
    mine = lax.select_n(z, *orders)
    position = lax.broadcasted_iota(jnp.int32, mine.shape, 0)
    lane = lax.broadcasted_iota(jnp.int32, mine.shape, 1)
    mine = jnp.where((lane < DH) | (position < lengths[0]), mine, 0)

    parts = [mine] + [along_y(mine, d) for d in steps[1:]]
    own = (kv, r0p, r0m, r1m, r0x, r1x, r1p, r2a, r2b)
    state = attend_own(info, query, own)
    parts, state = tie((parts, state))
    prompt = [part for value in parts for part in (value, swap(value))]
    return attend_prompt(info, query, state, prompt, own)[None]


def solution(mesh):
    placed = (P("grp", "hd", None), P("grp", "hd", None), P("grp", "hd", None), P())
    return jax.shard_map(
        on_device, mesh=mesh, in_specs=placed, out_specs=P("grp", "hd", None), check_vma=False
    )
```

```python
import math

import jax
import jax.numpy as jnp
from jax import lax
from jax.experimental import pallas as pl
from jax.experimental.pallas import tpu as pltpu
from jax.sharding import PartitionSpec as P

DH = 128
ROWS = 128
KVH = 8
GROUP = 8
PAIR = 2 * DH
SCALE_LOG2 = math.log2(math.e) / math.sqrt(DH)
NEG = -1e30
LEAST, MOST = 2.0**-80, 2.0**100
NT = (((1,), (1,)), ((), ()))
TILE = 256
IN_TILE = TILE // ROWS
PARAMS = pltpu.CompilerParams(vmem_limit_bytes=24 << 20)


def cost(heads, keys):
    pairs = GROUP * heads * ROWS * keys
    return pl.CostEstimate(flops=8 * pairs * DH, bytes_accessed=1 << 22, transcendentals=pairs)


def tiles(q_ref, head):
    for t in range(GROUP // IN_TILE):
        lanes = [lane_of(head, h) for h in range(t * IN_TILE, (t + 1) * IN_TILE)]
        yield t, jnp.concatenate([q_ref[:, lane] for lane in lanes], 0)


def lane_of(head, h):
    return pl.ds(pl.multiple_of((head * GROUP + h) * DH, DH), DH)


def causal_mask():
    row = lax.broadcasted_iota(jnp.int32, (TILE, ROWS), 0) % ROWS
    return row >= lax.broadcasted_iota(jnp.int32, (TILE, ROWS), 1)


def sweep(q_ref, head, k_scr, v_scr, n_keys, causal, put):
    for t, q in tiles(q_ref, head):
        s = lax.dot_general(q, k_scr[:n_keys, :], NT, preferred_element_type=jnp.float32)
        s = s * SCALE_LOG2
        if causal:
            s = jnp.concatenate([jnp.where(causal_mask(), s[:, :ROWS], NEG), s[:, ROWS:]], 1)
        p = jnp.exp2(s).astype(jnp.bfloat16)
        sums = jnp.dot(p, v_scr[:n_keys, :], preferred_element_type=jnp.float32)
        for j in range(IN_TILE):
            put(t * IN_TILE + j, sums[j * ROWS : (j + 1) * ROWS])


def place(k_scr, v_scr, slot, ref, ok):
    rows = slice(slot * ROWS, (slot + 1) * ROWS)
    k_scr[rows, :] = ref[:, :DH]
    v_scr[rows, :DH] = jnp.where(ok, ref[:, DH:], jnp.zeros_like(ref[:, DH:]))
    v_scr[rows, DH:] = jnp.where(ok, jnp.ones((ROWS, DH), jnp.float32), 0.0).astype(jnp.bfloat16)


def own_blocks(info):
    z, right = info[9], info[8] == 1
    return (True, z >= 1, z == 3, z >= 2, right, right, right, right)


def own_kernel(info, q_ref, *rest):
    blocks, (tot_ref, acc_ref, k_own, v_own) = rest[:9], rest[9:]
    head = pl.program_id(0)
    allowed = own_blocks(info)
    columns = pl.ds(pl.multiple_of(head * PAIR, PAIR), PAIR)
    half = pl.ds(pl.multiple_of(lax.rem(head, 4) * PAIR, PAIR), PAIR)

    @pl.when(info[11] > 0)
    def _():
        for slot in range(4):
            place(k_own, v_own, slot, blocks[slot][:, columns], allowed[slot])

        for slot in range(4, 7):
            place(k_own, v_own, slot, blocks[slot][:, columns], allowed[slot])

        @pl.when(head < 4)
        def _():
            place(k_own, v_own, 7, blocks[7][:, half], allowed[7])

        @pl.when(head >= 4)
        def _():
            place(k_own, v_own, 7, blocks[8][:, half], allowed[7])

        lane = lax.broadcasted_iota(jnp.int32, (ROWS, DH), 1)
        totals = []

        def put(h, sums):
            acc_ref[:, lane_of(head, h)] = sums[:, :DH]
            totals.append(jnp.where(lane == h, sums[:, DH:], totals[-1] if totals else 0.0))

        sweep(q_ref, head, k_own, v_own, 8 * ROWS, True, put)
        tot_ref[:, pl.ds(pl.multiple_of(head * DH, DH), DH)] = totals[-1]


def prompt_kernel(info, q_ref, tot_in, acc_in, *rest):
    prompt, stored, rest = rest[:KVH], rest[KVH : KVH + 9], rest[KVH + 9 :]
    o_ref, k_pre, v_pre, flag = rest[:4]
    step = pl.program_id(0)
    head = info[step]
    pre_len, n_live = info[10], info[11]
    chunks = (pre_len + 255) // 256
    row = lax.broadcasted_iota(jnp.int32, (ROWS, DH), 0)

    @pl.when(step == 0)
    def _():
        live = lax.broadcasted_iota(jnp.int32, (8 * ROWS, DH), 0) < pre_len
        v_pre[:, DH:] = jnp.where(live, 1.0, 0.0).astype(jnp.bfloat16)

    @pl.when(n_live > 0)
    def _():
        for n, buffer in enumerate(prompt):

            @pl.when(step == n)
            def _(buffer=buffer):
                k_pre[...] = buffer[:, :DH]
                v_pre[:, :DH] = buffer[:, DH:]

        flag[...] = jnp.zeros_like(flag)

        def finish(h, sums):
            totals = tot_in[:, pl.ds(pl.multiple_of(head * DH, DH), DH)]
            total = totals[:, h : h + 1]
            out = acc_in[:, lane_of(head, h)]
            if sums is None:
                total = jnp.broadcast_to(total, (ROWS, DH))
            else:
                total = total + sums[:, DH:]
                out = out + sums[:, :DH]
            wrong = jnp.where((total >= LEAST) & (total <= MOST), 0.0, 1.0)
            flag[...] = jnp.maximum(flag[...], jnp.where(row < n_live, wrong, 0.0))
            out = jnp.where(row < n_live, out / total, 0.0)
            o_ref[:, h * DH : (h + 1) * DH] = out.astype(jnp.bfloat16)

        @pl.when(chunks == 0)
        def _():
            for h in range(GROUP):
                finish(h, None)

        for n in range(1, 5):

            @pl.when(chunks == n)
            def _(n=n):
                sweep(q_ref, head, k_pre, v_pre, 256 * n, False, finish)

        @pl.when(jnp.max(flag[...]) > 0.5)
        def _():
            with_largest(info, head, q_ref, k_pre, v_pre, stored, o_ref, *rest[4:])

    @pl.when(n_live <= 0)
    def _():
        o_ref[...] = jnp.zeros_like(o_ref)


def with_largest(info, head, q_ref, k_pre, v_pre, stored, o_ref, k_aug, v_aug, land, sem):
    pre_len, n_live = info[10], info[11]
    allowed = own_blocks(info)

    def put(rows, count, key, value, ok):
        first = lax.broadcasted_iota(jnp.int32, (count, DH), 1) == 0
        k_aug[rows, :DH] = key
        k_aug[rows, DH:] = jnp.where(first & jnp.logical_not(ok), NEG, 0.0).astype(jnp.bfloat16)
        v_aug[rows, :DH] = value
        v_aug[rows, DH:] = jnp.ones((count, DH), jnp.bfloat16)

    def fetch(source, columns):
        copy = pltpu.make_async_copy(source.at[:, columns], land, sem)
        copy.start()
        copy.wait()

    columns = pl.ds(pl.multiple_of(head * PAIR, PAIR), PAIR)
    half = pl.ds(pl.multiple_of(lax.rem(head, 4) * PAIR, PAIR), PAIR)
    for slot in range(8):
        if slot < 7:
            fetch(stored[slot], columns)
        else:
            for low, source in ((True, stored[7]), (False, stored[8])):

                @pl.when((head < 4) == low)
                def _(source=source):
                    fetch(source, half)

        rows = slice(slot * ROWS, (slot + 1) * ROWS)
        put(rows, ROWS, land[:, :DH], land[:, DH:], allowed[slot])
    position = lax.broadcasted_iota(jnp.int32, (8 * ROWS, DH), 0)
    rows = slice(8 * ROWS, 16 * ROWS)
    put(rows, 8 * ROWS, k_pre[...], v_pre[:, :DH], position < pre_len)

    row = lax.broadcasted_iota(jnp.int32, (ROWS, PAIR), 0)
    col = lax.broadcasted_iota(jnp.int32, (ROWS, PAIR), 1)
    one = jnp.where(col[:, :DH] == 0, 1.0, 0.0).astype(jnp.bfloat16)

    @pl.loop(0, GROUP)
    def _(h):
        lane = pl.ds(pl.multiple_of(h * DH, DH), DH)
        q = jnp.concatenate([q_ref[:, lane_of(head, h)], one], 1)

        def scores(c):
            keys = pl.ds(pl.multiple_of(c * PAIR, PAIR), PAIR)
            s = lax.dot_general(q, k_aug[keys, :], NT, preferred_element_type=jnp.float32)
            return jnp.where((row >= col) | (col >= ROWS) | (c > 0), s, NEG), keys

        def largest(c, top):
            return jnp.maximum(top, jnp.max(scores(c)[0], axis=1, keepdims=True))

        top = lax.fori_loop(0, 8, largest, jnp.full((ROWS, 1), NEG, jnp.float32))

        def weigh(c, acc):
            s, keys = scores(c)
            p = jnp.exp2((s - top) * SCALE_LOG2).astype(jnp.bfloat16)
            return acc + jnp.dot(p, v_aug[keys, :], preferred_element_type=jnp.float32)

        acc = lax.fori_loop(0, 8, weigh, jnp.zeros((ROWS, PAIR), jnp.float32))
        out = jnp.where(row[:, :DH] < n_live, acc[:, :DH] / acc[:, DH:], 0.0)
        o_ref[:, lane] = out.astype(jnp.bfloat16)


VMEM = pl.BlockSpec(memory_space=pltpu.VMEM)
ANY = pl.BlockSpec(memory_space=pl.ANY)


def scratch():
    return [
        pltpu.VMEM((8 * ROWS, DH), jnp.bfloat16),
        pltpu.VMEM((8 * ROWS, PAIR), jnp.bfloat16),
    ]


def attend_own(info, query, own):
    return pl.pallas_call(
        own_kernel,
        grid_spec=pltpu.PrefetchScalarGridSpec(
            num_scalar_prefetch=1,
            grid=(KVH,),
            in_specs=[VMEM] * (1 + len(own)),
            out_specs=(VMEM, VMEM),
            scratch_shapes=scratch(),
        ),
        out_shape=(
            jax.ShapeDtypeStruct((ROWS, KVH * DH), jnp.float32),
            jax.ShapeDtypeStruct((ROWS, KVH * GROUP * DH), jnp.float32),
        ),
        compiler_params=PARAMS,
        cost_estimate=cost(KVH, 8 * ROWS),
        name="own",
    )(info, query, *own)


def attend_prompt(info, query, state, prompt, own):
    return pl.pallas_call(
        prompt_kernel,
        grid_spec=pltpu.PrefetchScalarGridSpec(
            num_scalar_prefetch=1,
            grid=(KVH,),
            in_specs=[VMEM] * (3 + len(prompt)) + [ANY] * len(own),
            out_specs=pl.BlockSpec((ROWS, GROUP * DH), lambda i, info: (0, info[i])),
            scratch_shapes=scratch()
            + [
                pltpu.VMEM((ROWS, DH), jnp.float32),
                pltpu.VMEM((16 * ROWS, PAIR), jnp.bfloat16),
                pltpu.VMEM((16 * ROWS, PAIR), jnp.bfloat16),
                pltpu.VMEM((ROWS, PAIR), jnp.bfloat16),
                pltpu.SemaphoreType.DMA(()),
            ],
        ),
        out_shape=jax.ShapeDtypeStruct(query.shape, jnp.bfloat16),
        compiler_params=PARAMS,
        cost_estimate=cost(KVH, 8 * ROWS),
        name="prompt",
    )(info, query, *state, *prompt, *own)


def pair_kernel(k_ref, v_ref, o_ref, top_ref):
    for h in range(KVH):
        o_ref[:, h * PAIR : h * PAIR + DH] = k_ref[:, h * DH : (h + 1) * DH]
        o_ref[:, h * PAIR + DH : (h + 1) * PAIR] = v_ref[:, h * DH : (h + 1) * DH]
    top_ref[...] = o_ref[:, 4 * PAIR :]


def pair_up(keys, values):
    return pl.pallas_call(
        pair_kernel,
        out_shape=(
            jax.ShapeDtypeStruct((ROWS, KVH * PAIR), jnp.bfloat16),
            jax.ShapeDtypeStruct((ROWS, 4 * PAIR), jnp.bfloat16),
        ),
    )(keys, values)


def on_device(query_rows, key_rows, value_rows, lengths):
    grp = lax.axis_index("grp")
    hd = lax.axis_index("hd")
    core, y, x_lo = grp % 2, (grp // 2) % 4, grp // 8
    z, x_hi = hd % 4, hd // 4
    query = query_rows[0]
    kv, top = pair_up(key_rows[0], value_rows[0])

    def on_hd(value, pairs):
        return lax.ppermute(value, "hd", pairs)

    def on_grp(value, pairs):
        return lax.ppermute(value, "grp", pairs)

    def along_y(value, d):
        return on_grp(value, [(g, (g & 9) | ((g + 2 * d) & 6)) for g in range(16)])

    def along_z(value, d):
        return on_hd(value, [(4 * x + i, 4 * x + (i + d) % 4) for x in range(2) for i in range(4)])

    def swap(value):
        return on_grp(value, [(g, g ^ 1) for g in range(16)])

    def along_x_hi(value):
        return on_hd(value, [(i, i ^ 4) for i in range(8)])

    tie = lax.optimization_barrier

    steps = (0, 1, 3, 2)
    heads = [4 * c + (y - d) % 4 for d in steps for c in (core, 1 - core)]
    pre_len = jnp.where(grp == 0, 0, lengths[0])
    n_live = lengths[grp] - hd * ROWS
    info = jnp.stack([jnp.int32(v) for v in heads + [x_hi, z, pre_len, n_live]])

    r0x, r0p, r0m = along_x_hi(kv), along_z(kv, 1), along_z(kv, 3)
    four = jnp.where(core == 0, kv[:, : 4 * PAIR], swap(top))
    one = four[:, :PAIR]
    for d in range(1, 4):
        one = jnp.where(y == d, along_y(four[:, d * PAIR : (d + 1) * PAIR], d), one)
    r0x, r0p, r0m, one = tie((r0x, r0p, r0m, one))

    piece = jnp.where(x_lo == 0, one, on_grp(one, [(g, g ^ 8) for g in range(16)]))
    other, r0x_t, r0m_t = tie((along_x_hi(piece), r0x, r0m))
    both = jnp.stack(
        [jnp.where(x_hi == 0, piece, other), jnp.where(x_hi == 0, other, piece)]
    )

    r1x, r1p, r1m = along_x_hi(r0m_t), along_z(r0x_t, 1), along_z(r0m_t, 3)
    r2a, r2b = along_x_hi(r1m[:, : 4 * PAIR]), along_z(r1p[:, 4 * PAIR :], 1)
    behind = [both] + [along_z(both, d) for d in range(1, 4)]
    orders = [
        jnp.stack([behind[(at - i) % 4] for i in range(4)], 1).reshape(8 * ROWS, PAIR)
        for at in range(4)
    ]
    mine = lax.select_n(z, *orders)
    position = lax.broadcasted_iota(jnp.int32, mine.shape, 0)
    lane = lax.broadcasted_iota(jnp.int32, mine.shape, 1)
    mine = jnp.where((lane < DH) | (position < lengths[0]), mine, 0)

    m, e1, e3, e2 = [mine] + [along_y(mine, d) for d in steps[1:]]
    own = (kv, r0p, r0m, r1m, r0x, r1x, r1p, r2a, r2b)
    state = attend_own(info, query, own)
    (m, e1, e3, e2), state = tie(((m, e1, e3, e2), state))
    prompt = [part for value in (m, e1, e3, e2) for part in (value, swap(value))]
    return attend_prompt(info, query, state, prompt, own)[None]


def solution(mesh):
    placed = (P("grp", "hd", None), P("grp", "hd", None), P("grp", "hd", None), P())
    return jax.shard_map(
        on_device, mesh=mesh, in_specs=placed, out_specs=P("grp", "hd", None), check_vma=False
    )
```

```python
import functools
import math

import jax
import jax.numpy as jnp
from jax import lax
from jax.experimental import pallas as pl
from jax.experimental.pallas import tpu as pltpu
from jax.sharding import PartitionSpec as P

DH = 128
ROWS = 128
KVH = 8
GROUP = 8
PAIR = 2 * DH
SCALE_LOG2 = math.log2(math.e) / math.sqrt(DH)
NEG = -1e30
LEAST, MOST = 2.0**-80, 2.0**100
NT = (((1,), (1,)), ((), ()))
TILE = 256
IN_TILE = TILE // ROWS
PARAMS = pltpu.CompilerParams(vmem_limit_bytes=24 << 20)


def cost(heads, keys):
    pairs = GROUP * heads * ROWS * keys
    return pl.CostEstimate(flops=8 * pairs * DH, bytes_accessed=1 << 22, transcendentals=pairs)


def tiles(q_ref, head):
    for t in range(GROUP // IN_TILE):
        lanes = [lane_of(head, h) for h in range(t * IN_TILE, (t + 1) * IN_TILE)]
        yield t, jnp.concatenate([q_ref[:, lane] for lane in lanes], 0)


def lane_of(head, h):
    return pl.ds(pl.multiple_of((head * GROUP + h) * DH, DH), DH)


def causal_mask():
    row = lax.broadcasted_iota(jnp.int32, (TILE, ROWS), 0) % ROWS
    return row >= lax.broadcasted_iota(jnp.int32, (TILE, ROWS), 1)


def sweep(q_ref, head, k_scr, v_scr, n_keys, causal, put):
    for t, q in tiles(q_ref, head):
        s = lax.dot_general(q, k_scr[:n_keys, :], NT, preferred_element_type=jnp.float32)
        s = s * SCALE_LOG2
        if causal:
            s = jnp.concatenate([jnp.where(causal_mask(), s[:, :ROWS], NEG), s[:, ROWS:]], 1)
        p = jnp.exp2(s).astype(jnp.bfloat16)
        sums = jnp.dot(p, v_scr[:n_keys, :], preferred_element_type=jnp.float32)
        for j in range(IN_TILE):
            put(t * IN_TILE + j, sums[j * ROWS : (j + 1) * ROWS])


def place(k_scr, v_scr, slot, ref, ok):
    rows = slice(slot * ROWS, (slot + 1) * ROWS)
    k_scr[rows, :] = ref[:, :DH]
    v_scr[rows, :DH] = jnp.where(ok, ref[:, DH:], jnp.zeros_like(ref[:, DH:]))
    v_scr[rows, DH:] = jnp.where(ok, jnp.ones((ROWS, DH), jnp.float32), 0.0).astype(jnp.bfloat16)


def own_blocks(info):
    z, right = info[9], info[8] == 1
    return (True, z >= 1, z == 3, z >= 2, right, right, right, right)


def own_kernel(info, q_ref, *rest):
    blocks, (tot_ref, acc_ref, k_own, v_own) = rest[:9], rest[9:]
    head = pl.program_id(0)
    allowed = own_blocks(info)
    columns = pl.ds(pl.multiple_of(head * PAIR, PAIR), PAIR)
    half = pl.ds(pl.multiple_of(lax.rem(head, 4) * PAIR, PAIR), PAIR)

    @pl.when(info[11] > 0)
    def _():
        for slot in range(4):
            place(k_own, v_own, slot, blocks[slot][:, columns], allowed[slot])

        for slot in range(4, 7):
            place(k_own, v_own, slot, blocks[slot][:, columns], allowed[slot])

        @pl.when(head < 4)
        def _():
            place(k_own, v_own, 7, blocks[7][:, half], allowed[7])

        @pl.when(head >= 4)
        def _():
            place(k_own, v_own, 7, blocks[8][:, half], allowed[7])

        lane = lax.broadcasted_iota(jnp.int32, (ROWS, DH), 1)

        def run(n_keys):
            totals = []

            def put(h, sums):
                acc_ref[:, lane_of(head, h)] = sums[:, :DH]
                totals.append(jnp.where(lane == h, sums[:, DH:], totals[-1] if totals else 0.0))

            sweep(q_ref, head, k_own, v_own, n_keys, True, put)
            tot_ref[:, pl.ds(pl.multiple_of(head * DH, DH), DH)] = totals[-1]

        @pl.when(info[8] == 1)
        def _():
            run(8 * ROWS)

        @pl.when(info[8] == 0)
        def _():
            run(4 * ROWS)


def prompt_kernel(first, count, aliased, info, q_ref, tot_in, acc_in, *rest):
    prompt, stored, rest = rest[:count], rest[count : count + 9], rest[count + 9 + aliased :]
    o_hbm, k_pre, v_pre, out, flags, sems = rest[:6]
    pre_len, n_live = info[10], info[11]
    chunks = (pre_len + 255) // 256
    row = lax.broadcasted_iota(jnp.int32, (ROWS, DH), 0)

    def store(i):
        columns = pl.ds(pl.multiple_of(info[first + i] * GROUP * DH, GROUP * DH), GROUP * DH)
        return pltpu.make_async_copy(out.at[i], o_hbm.at[:, columns], sems.at[i])

    def take(i):
        for n, buffer in enumerate(prompt):

            @pl.when(i == n)
            def _(buffer=buffer):
                k_pre[...] = buffer[:, :DH]
                v_pre[:, :DH] = buffer[:, DH:]

    def attend(n_keys):
        @pl.loop(0, count)
        def _(i):
            head = info[first + i]
            take(i)
            flags[i] = jnp.zeros((ROWS, DH), jnp.float32)

            def finish(h, sums):
                totals = tot_in[:, pl.ds(pl.multiple_of(head * DH, DH), DH)]
                total = totals[:, h : h + 1]
                value = acc_in[:, lane_of(head, h)]
                if sums is None:
                    total = jnp.broadcast_to(total, (ROWS, DH))
                else:
                    total = total + sums[:, DH:]
                    value = value + sums[:, :DH]
                wrong = jnp.where((total >= LEAST) & (total <= MOST), 0.0, 1.0)
                flags[i] = jnp.maximum(flags[i], jnp.where(row < n_live, wrong, 0.0))
                value = jnp.where(row < n_live, value / total, 0.0)
                out[i, :, h * DH : (h + 1) * DH] = value.astype(jnp.bfloat16)

            if n_keys == 0:
                for h in range(GROUP):
                    finish(h, None)
            else:
                sweep(q_ref, head, k_pre, v_pre, n_keys, False, finish)
            store(i).start()

    @pl.when(n_live > 0)
    def _():
        live = lax.broadcasted_iota(jnp.int32, (8 * ROWS, DH), 0) < pre_len
        v_pre[:, DH:] = jnp.where(live, 1.0, 0.0).astype(jnp.bfloat16)
        for n in (0, 2, 3, 4):

            @pl.when((chunks == n) | ((n == 2) & (chunks == 1)))
            def _(n=n):
                attend(256 * n)

    @pl.when(n_live <= 0)
    def _():
        out[...] = jnp.zeros_like(out)
        for i in range(count):
            store(i).start()

    for i in range(count):
        store(i).wait()

    @pl.when(n_live > 0)
    def _():
        @pl.when(jnp.max(flags[...]) > 0.5)
        def _():
            @pl.loop(0, count)
            def _(i):
                @pl.when(jnp.max(flags[i]) > 0.5)
                def _():
                    take(i)
                    with_largest(
                        info, info[first + i], q_ref, k_pre, v_pre, stored, out.at[i], *rest[6:]
                    )
                    store(i).start()
                    store(i).wait()


def with_largest(info, head, q_ref, k_pre, v_pre, stored, o_ref, k_aug, v_aug, land, sem):
    pre_len, n_live = info[10], info[11]
    allowed = own_blocks(info)

    def put(rows, count, key, value, ok):
        first = lax.broadcasted_iota(jnp.int32, (count, DH), 1) == 0
        k_aug[rows, :DH] = key
        k_aug[rows, DH:] = jnp.where(first & jnp.logical_not(ok), NEG, 0.0).astype(jnp.bfloat16)
        v_aug[rows, :DH] = value
        v_aug[rows, DH:] = jnp.ones((count, DH), jnp.bfloat16)

    def fetch(source, columns):
        copy = pltpu.make_async_copy(source.at[:, columns], land, sem)
        copy.start()
        copy.wait()

    columns = pl.ds(pl.multiple_of(head * PAIR, PAIR), PAIR)
    half = pl.ds(pl.multiple_of(lax.rem(head, 4) * PAIR, PAIR), PAIR)
    for slot in range(8):
        if slot < 7:
            fetch(stored[slot], columns)
        else:
            for low, source in ((True, stored[7]), (False, stored[8])):

                @pl.when((head < 4) == low)
                def _(source=source):
                    fetch(source, half)

        rows = slice(slot * ROWS, (slot + 1) * ROWS)
        put(rows, ROWS, land[:, :DH], land[:, DH:], allowed[slot])
    position = lax.broadcasted_iota(jnp.int32, (8 * ROWS, DH), 0)
    rows = slice(8 * ROWS, 16 * ROWS)
    put(rows, 8 * ROWS, k_pre[...], v_pre[:, :DH], position < pre_len)

    row = lax.broadcasted_iota(jnp.int32, (ROWS, PAIR), 0)
    col = lax.broadcasted_iota(jnp.int32, (ROWS, PAIR), 1)
    one = jnp.where(col[:, :DH] == 0, 1.0, 0.0).astype(jnp.bfloat16)

    @pl.loop(0, GROUP)
    def _(h):
        lane = pl.ds(pl.multiple_of(h * DH, DH), DH)
        q = jnp.concatenate([q_ref[:, lane_of(head, h)], one], 1)

        def scores(c):
            keys = pl.ds(pl.multiple_of(c * PAIR, PAIR), PAIR)
            s = lax.dot_general(q, k_aug[keys, :], NT, preferred_element_type=jnp.float32)
            return jnp.where((row >= col) | (col >= ROWS) | (c > 0), s, NEG), keys

        def largest(c, top):
            return jnp.maximum(top, jnp.max(scores(c)[0], axis=1, keepdims=True))

        top = lax.fori_loop(0, 8, largest, jnp.full((ROWS, 1), NEG, jnp.float32))

        def weigh(c, acc):
            s, keys = scores(c)
            p = jnp.exp2((s - top) * SCALE_LOG2).astype(jnp.bfloat16)
            return acc + jnp.dot(p, v_aug[keys, :], preferred_element_type=jnp.float32)

        acc = lax.fori_loop(0, 8, weigh, jnp.zeros((ROWS, PAIR), jnp.float32))
        out = jnp.where(row[:, :DH] < n_live, acc[:, :DH] / acc[:, DH:], 0.0)
        o_ref[:, lane] = out.astype(jnp.bfloat16)


VMEM = pl.BlockSpec(memory_space=pltpu.VMEM)
ANY = pl.BlockSpec(memory_space=pl.ANY)


def scratch():
    return [
        pltpu.VMEM((8 * ROWS, DH), jnp.bfloat16),
        pltpu.VMEM((8 * ROWS, PAIR), jnp.bfloat16),
    ]


def attend_own(info, query, own):
    return pl.pallas_call(
        own_kernel,
        grid_spec=pltpu.PrefetchScalarGridSpec(
            num_scalar_prefetch=1,
            grid=(KVH,),
            in_specs=[VMEM] * (1 + len(own)),
            out_specs=(VMEM, VMEM),
            scratch_shapes=scratch(),
        ),
        out_shape=(
            jax.ShapeDtypeStruct((ROWS, KVH * DH), jnp.float32),
            jax.ShapeDtypeStruct((ROWS, KVH * GROUP * DH), jnp.float32),
        ),
        compiler_params=PARAMS,
        cost_estimate=cost(KVH, 8 * ROWS),
        name="own",
    )(info, query, *own)


def attend_prompt(info, query, state, prompt, own, first, before):
    last = () if before is None else (before,)
    operands = (info, query, *state, *prompt, *own, *last)
    count = len(prompt)
    return pl.pallas_call(
        functools.partial(prompt_kernel, first, count, len(last)),
        grid_spec=pltpu.PrefetchScalarGridSpec(
            num_scalar_prefetch=1,
            grid=(1,),
            in_specs=[VMEM] * (3 + count) + [ANY] * (len(own) + len(last)),
            out_specs=ANY,
            scratch_shapes=scratch()
            + [
                pltpu.VMEM((count, ROWS, GROUP * DH), jnp.bfloat16),
                pltpu.VMEM((count, ROWS, DH), jnp.float32),
                pltpu.SemaphoreType.DMA((count,)),
                pltpu.VMEM((16 * ROWS, PAIR), jnp.bfloat16),
                pltpu.VMEM((16 * ROWS, PAIR), jnp.bfloat16),
                pltpu.VMEM((ROWS, PAIR), jnp.bfloat16),
                pltpu.SemaphoreType.DMA(()),
            ],
        ),
        out_shape=jax.ShapeDtypeStruct(query.shape, jnp.bfloat16),
        input_output_aliases={} if before is None else {len(operands) - 1: 0},
        compiler_params=PARAMS,
        cost_estimate=cost(count, 8 * ROWS),
        name=f"prompt{first}",
    )(*operands)


def pair_kernel(k_ref, v_ref, o_ref, top_ref):
    for h in range(KVH):
        o_ref[:, h * PAIR : h * PAIR + DH] = k_ref[:, h * DH : (h + 1) * DH]
        o_ref[:, h * PAIR + DH : (h + 1) * PAIR] = v_ref[:, h * DH : (h + 1) * DH]
    top_ref[...] = o_ref[:, 4 * PAIR :]


def pair_up(keys, values):
    return pl.pallas_call(
        pair_kernel,
        out_shape=(
            jax.ShapeDtypeStruct((ROWS, KVH * PAIR), jnp.bfloat16),
            jax.ShapeDtypeStruct((ROWS, 4 * PAIR), jnp.bfloat16),
        ),
    )(keys, values)


def on_device(query_rows, key_rows, value_rows, lengths):
    grp = lax.axis_index("grp")
    hd = lax.axis_index("hd")
    core, y, x_lo = grp % 2, (grp // 2) % 4, grp // 8
    z, x_hi = hd % 4, hd // 4
    query = query_rows[0]
    kv, top = pair_up(key_rows[0], value_rows[0])

    def on_hd(value, pairs):
        return lax.ppermute(value, "hd", pairs)

    def on_grp(value, pairs):
        return lax.ppermute(value, "grp", pairs)

    def along_y(value, d):
        return on_grp(value, [(g, (g & 9) | ((g + 2 * d) & 6)) for g in range(16)])

    def along_z(value, d):
        return on_hd(value, [(4 * x + i, 4 * x + (i + d) % 4) for x in range(2) for i in range(4)])

    def swap(value):
        return on_grp(value, [(g, g ^ 1) for g in range(16)])

    def along_x_hi(value):
        return on_hd(value, [(i, i ^ 4) for i in range(8)])

    tie = lax.optimization_barrier

    steps = (0, 1, 3, 2)
    heads = [4 * c + (y - d) % 4 for c in (core, 1 - core) for d in steps]
    pre_len = jnp.where(grp == 0, 0, lengths[0])
    n_live = lengths[grp] - hd * ROWS
    info = jnp.stack([jnp.int32(v) for v in heads + [x_hi, z, pre_len, n_live]])

    r0x, r0p, r0m = along_x_hi(kv), along_z(kv, 1), along_z(kv, 3)
    four = jnp.where(core == 0, kv[:, : 4 * PAIR], swap(top))
    one = four[:, :PAIR]
    for d in range(1, 4):
        one = jnp.where(y == d, along_y(four[:, d * PAIR : (d + 1) * PAIR], d), one)
    r0x, r0p, r0m, one = tie((r0x, r0p, r0m, one))

    piece = jnp.where(x_lo == 0, one, on_grp(one, [(g, g ^ 8) for g in range(16)]))
    other, r0x_t, r0m_t = tie((along_x_hi(piece), r0x, r0m))
    both = jnp.stack(
        [jnp.where(x_hi == 0, piece, other), jnp.where(x_hi == 0, other, piece)]
    )

    r1x, r1p, r1m = along_x_hi(r0m_t), along_z(r0x_t, 1), along_z(r0m_t, 3)
    r2a, r2b = along_x_hi(r1m[:, : 4 * PAIR]), along_z(r1p[:, 4 * PAIR :], 1)
    behind = [both] + [along_z(both, d) for d in range(1, 4)]
    orders = [
        jnp.stack([behind[(at - i) % 4] for i in range(4)], 1).reshape(8 * ROWS, PAIR)
        for at in range(4)
    ]
    mine = lax.select_n(z, *orders)
    position = lax.broadcasted_iota(jnp.int32, mine.shape, 0)
    lane = lax.broadcasted_iota(jnp.int32, mine.shape, 1)
    mine = jnp.where((lane < DH) | (position < lengths[0]), mine, 0)

    parts = [mine] + [along_y(mine, d) for d in steps[1:]]
    own = (kv, r0p, r0m, r1m, r0x, r1x, r1p, r2a, r2b)
    state = attend_own(info, query, own)
    parts, state = tie((parts, state))
    swapped = [swap(value) for value in parts]
    out = attend_prompt(info, query, state, parts, own, 0, None)
    return attend_prompt(info, query, state, swapped, own, 4, out)[None]


def solution(mesh):
    placed = (P("grp", "hd", None), P("grp", "hd", None), P("grp", "hd", None), P())
    return jax.shard_map(
        on_device, mesh=mesh, in_specs=placed, out_specs=P("grp", "hd", None), check_vma=False
    )
```

```python
import functools
import math

import jax
import jax.numpy as jnp
from jax import lax
from jax.experimental import pallas as pl
from jax.experimental.pallas import tpu as pltpu
from jax.sharding import PartitionSpec as P

DH = 128
ROWS = 128
KVH = 8
GROUP = 8
PAIR = 2 * DH
SCALE_LOG2 = math.log2(math.e) / math.sqrt(DH)
NEG = -1e30
LEAST, MOST = 2.0**-80, 2.0**100
NT = (((1,), (1,)), ((), ()))
TILE = 256
IN_TILE = TILE // ROWS
PARAMS = pltpu.CompilerParams(vmem_limit_bytes=24 << 20)


def cost(heads, keys):
    pairs = GROUP * heads * ROWS * keys
    return pl.CostEstimate(flops=8 * pairs * DH, bytes_accessed=1 << 22, transcendentals=pairs)


def tiles(q_ref, head):
    for t in range(GROUP // IN_TILE):
        lanes = [lane_of(head, h) for h in range(t * IN_TILE, (t + 1) * IN_TILE)]
        yield t, jnp.concatenate([q_ref[:, lane] for lane in lanes], 0)


def lane_of(head, h):
    return pl.ds(pl.multiple_of((head * GROUP + h) * DH, DH), DH)


def causal_mask():
    row = lax.broadcasted_iota(jnp.int32, (TILE, ROWS), 0) % ROWS
    return row >= lax.broadcasted_iota(jnp.int32, (TILE, ROWS), 1)


def sweep(q_ref, head, k_scr, v_scr, n_keys, causal, put):
    for t, q in tiles(q_ref, head):
        s = lax.dot_general(q, k_scr[:n_keys, :], NT, preferred_element_type=jnp.float32)
        s = s * SCALE_LOG2
        if causal:
            s = jnp.concatenate([jnp.where(causal_mask(), s[:, :ROWS], NEG), s[:, ROWS:]], 1)
        p = jnp.exp2(s).astype(jnp.bfloat16)
        sums = jnp.dot(p, v_scr[:n_keys, :], preferred_element_type=jnp.float32)
        for j in range(IN_TILE):
            put(t * IN_TILE + j, sums[j * ROWS : (j + 1) * ROWS])


def place(k_scr, v_scr, slot, ref, ok):
    rows = slice(slot * ROWS, (slot + 1) * ROWS)
    k_scr[rows, :] = ref[:, :DH]
    v_scr[rows, :DH] = jnp.where(ok, ref[:, DH:], jnp.zeros_like(ref[:, DH:]))
    v_scr[rows, DH:] = jnp.where(ok, jnp.ones((ROWS, DH), jnp.float32), 0.0).astype(jnp.bfloat16)


def own_blocks(info):
    z, right = info[9], info[8] == 1
    return (True, z >= 1, z == 3, z >= 2, right, right, right, right)


def own_kernel(info, q_ref, *rest):
    blocks, (tot_ref, acc_ref, k_own, v_own) = rest[:9], rest[9:]
    head = pl.program_id(0)
    allowed = own_blocks(info)
    columns = pl.ds(pl.multiple_of(head * PAIR, PAIR), PAIR)

    @pl.when(info[11] > 0)
    def _():
        for slot in range(7):
            place(k_own, v_own, slot, blocks[slot][:, columns], allowed[slot])
        last = jnp.concatenate([blocks[7][:, columns], blocks[8][:, columns]], 0)
        place(k_own, v_own, 7, last, allowed[7])
        lane = lax.broadcasted_iota(jnp.int32, (ROWS, DH), 1)

        def run(n_keys):
            totals = []

            def put(h, sums):
                acc_ref[:, lane_of(head, h)] = sums[:, :DH]
                totals.append(jnp.where(lane == h, sums[:, DH:], totals[-1] if totals else 0.0))

            sweep(q_ref, head, k_own, v_own, n_keys, True, put)
            tot_ref[:, pl.ds(pl.multiple_of(head * DH, DH), DH)] = totals[-1]

        @pl.when(info[8] == 1)
        def _():
            run(8 * ROWS)

        @pl.when(info[8] == 0)
        def _():
            run(4 * ROWS)


def prompt_kernel(first, count, aliased, info, q_ref, tot_in, acc_in, *rest):
    prompt, stored, rest = rest[:count], rest[count : count + 9], rest[count + 9 + aliased :]
    o_hbm, k_pre, v_pre, out, flags, sems = rest[:6]
    pre_len, n_live = info[10], info[11]
    chunks = (pre_len + 255) // 256
    row = lax.broadcasted_iota(jnp.int32, (ROWS, DH), 0)

    def store(i):
        columns = pl.ds(pl.multiple_of(info[first + i] * GROUP * DH, GROUP * DH), GROUP * DH)
        return pltpu.make_async_copy(out.at[i], o_hbm.at[:, columns], sems.at[i])

    def take(i):
        for n, buffer in enumerate(prompt):

            @pl.when(i == n)
            def _(buffer=buffer):
                k_pre[...] = buffer[:, :DH]
                v_pre[:, :DH] = buffer[:, DH:]

    def attend(n_keys):
        @pl.loop(0, count)
        def _(i):
            head = info[first + i]
            take(i)
            lane = lax.broadcasted_iota(jnp.int32, (ROWS, DH), 1)
            own_totals = tot_in[:, pl.ds(pl.multiple_of(head * DH, DH), DH)]
            totals = [jnp.ones((ROWS, DH), jnp.float32)]

            def finish(h, sums):
                total = own_totals[:, h : h + 1]
                value = acc_in[:, lane_of(head, h)]
                if sums is None:
                    total = jnp.broadcast_to(total, (ROWS, DH))
                else:
                    total = total + sums[:, DH:]
                    value = value + sums[:, :DH]
                totals.append(jnp.where(lane == h, total, totals[-1]))
                scale = pl.reciprocal(total, approx=True)
                scale = scale * (2.0 - total * scale)
                value = jnp.where(row < n_live, value * scale, 0.0)
                out[i, :, h * DH : (h + 1) * DH] = value.astype(jnp.bfloat16)

            if n_keys == 0:
                for h in range(GROUP):
                    finish(h, None)
            else:
                sweep(q_ref, head, k_pre, v_pre, n_keys, False, finish)
            store(i).start()
            fine = (totals[-1] >= LEAST) & (totals[-1] <= MOST)
            flags[i] = jnp.where(fine | (row >= n_live), 0.0, 1.0)

    @pl.when(n_live > 0)
    def _():
        live = lax.broadcasted_iota(jnp.int32, (8 * ROWS, DH), 0) < pre_len
        v_pre[:, DH:] = jnp.where(live, 1.0, 0.0).astype(jnp.bfloat16)
        for n in (0, 2, 3, 4):

            @pl.when((chunks == n) | ((n == 2) & (chunks == 1)))
            def _(n=n):
                attend(256 * n)

    @pl.when(n_live <= 0)
    def _():
        out[...] = jnp.zeros_like(out)
        for i in range(count):
            store(i).start()

    for i in range(count):
        store(i).wait()

    @pl.when(n_live > 0)
    def _():
        @pl.when(jnp.max(flags[...]) > 0.5)
        def _():
            @pl.loop(0, count)
            def _(i):
                @pl.when(jnp.max(flags[i]) > 0.5)
                def _():
                    take(i)
                    with_largest(
                        info, info[first + i], q_ref, k_pre, v_pre, stored, out.at[i], *rest[6:]
                    )
                    store(i).start()
                    store(i).wait()


def with_largest(info, head, q_ref, k_pre, v_pre, stored, o_ref, k_aug, v_aug, land, sem):
    pre_len, n_live = info[10], info[11]
    allowed = own_blocks(info)

    def put(rows, count, key, value, ok):
        first = lax.broadcasted_iota(jnp.int32, (count, DH), 1) == 0
        k_aug[rows, :DH] = key
        k_aug[rows, DH:] = jnp.where(first & jnp.logical_not(ok), NEG, 0.0).astype(jnp.bfloat16)
        v_aug[rows, :DH] = value
        v_aug[rows, DH:] = jnp.ones((count, DH), jnp.bfloat16)

    def fetch(source, target):
        columns = pl.ds(pl.multiple_of(head * PAIR, PAIR), PAIR)
        copy = pltpu.make_async_copy(source.at[:, columns], target, sem)
        copy.start()
        copy.wait()

    for slot in range(8):
        if slot < 7:
            fetch(stored[slot], land)
        else:
            fetch(stored[7], land.at[: ROWS // 2, :])
            fetch(stored[8], land.at[ROWS // 2 :, :])
        rows = slice(slot * ROWS, (slot + 1) * ROWS)
        put(rows, ROWS, land[:, :DH], land[:, DH:], allowed[slot])
    position = lax.broadcasted_iota(jnp.int32, (8 * ROWS, DH), 0)
    rows = slice(8 * ROWS, 16 * ROWS)
    put(rows, 8 * ROWS, k_pre[...], v_pre[:, :DH], position < pre_len)

    row = lax.broadcasted_iota(jnp.int32, (ROWS, PAIR), 0)
    col = lax.broadcasted_iota(jnp.int32, (ROWS, PAIR), 1)
    one = jnp.where(col[:, :DH] == 0, 1.0, 0.0).astype(jnp.bfloat16)

    @pl.loop(0, GROUP)
    def _(h):
        lane = pl.ds(pl.multiple_of(h * DH, DH), DH)
        q = jnp.concatenate([q_ref[:, lane_of(head, h)], one], 1)

        def scores(c):
            keys = pl.ds(pl.multiple_of(c * PAIR, PAIR), PAIR)
            s = lax.dot_general(q, k_aug[keys, :], NT, preferred_element_type=jnp.float32)
            return jnp.where((row >= col) | (col >= ROWS) | (c > 0), s, NEG), keys

        def largest(c, top):
            return jnp.maximum(top, jnp.max(scores(c)[0], axis=1, keepdims=True))

        top = lax.fori_loop(0, 8, largest, jnp.full((ROWS, 1), NEG, jnp.float32))

        def weigh(c, acc):
            s, keys = scores(c)
            p = jnp.exp2((s - top) * SCALE_LOG2).astype(jnp.bfloat16)
            return acc + jnp.dot(p, v_aug[keys, :], preferred_element_type=jnp.float32)

        acc = lax.fori_loop(0, 8, weigh, jnp.zeros((ROWS, PAIR), jnp.float32))
        out = jnp.where(row[:, :DH] < n_live, acc[:, :DH] / acc[:, DH:], 0.0)
        o_ref[:, lane] = out.astype(jnp.bfloat16)


VMEM = pl.BlockSpec(memory_space=pltpu.VMEM)
ANY = pl.BlockSpec(memory_space=pl.ANY)


def scratch():
    return [
        pltpu.VMEM((8 * ROWS, DH), jnp.bfloat16),
        pltpu.VMEM((8 * ROWS, PAIR), jnp.bfloat16),
    ]


def attend_own(info, query, own):
    return pl.pallas_call(
        own_kernel,
        grid_spec=pltpu.PrefetchScalarGridSpec(
            num_scalar_prefetch=1,
            grid=(KVH,),
            in_specs=[VMEM] * (1 + len(own)),
            out_specs=(VMEM, VMEM),
            scratch_shapes=scratch(),
        ),
        out_shape=(
            jax.ShapeDtypeStruct((ROWS, KVH * DH), jnp.float32),
            jax.ShapeDtypeStruct((ROWS, KVH * GROUP * DH), jnp.float32),
        ),
        compiler_params=PARAMS,
        cost_estimate=cost(KVH, 8 * ROWS),
        name="own",
    )(info, query, *own)


def attend_prompt(info, query, state, prompt, own, first, before):
    last = () if before is None else (before,)
    operands = (info, query, *state, *prompt, *own, *last)
    count = len(prompt)
    return pl.pallas_call(
        functools.partial(prompt_kernel, first, count, len(last)),
        grid_spec=pltpu.PrefetchScalarGridSpec(
            num_scalar_prefetch=1,
            grid=(1,),
            in_specs=[VMEM] * (3 + count) + [ANY] * (len(own) + len(last)),
            out_specs=ANY,
            scratch_shapes=scratch()
            + [
                pltpu.VMEM((count, ROWS, GROUP * DH), jnp.bfloat16),
                pltpu.VMEM((count, ROWS, DH), jnp.float32),
                pltpu.SemaphoreType.DMA((count,)),
                pltpu.VMEM((16 * ROWS, PAIR), jnp.bfloat16),
                pltpu.VMEM((16 * ROWS, PAIR), jnp.bfloat16),
                pltpu.VMEM((ROWS, PAIR), jnp.bfloat16),
                pltpu.SemaphoreType.DMA(()),
            ],
        ),
        out_shape=jax.ShapeDtypeStruct(query.shape, jnp.bfloat16),
        input_output_aliases={} if before is None else {len(operands) - 1: 0},
        compiler_params=PARAMS,
        cost_estimate=cost(count, 8 * ROWS),
        name=f"prompt{first}",
    )(*operands)


def pair_kernel(k_ref, v_ref, o_ref, top_ref):
    for h in range(KVH):
        o_ref[:, h * PAIR : h * PAIR + DH] = k_ref[:, h * DH : (h + 1) * DH]
        o_ref[:, h * PAIR + DH : (h + 1) * PAIR] = v_ref[:, h * DH : (h + 1) * DH]
    top_ref[...] = o_ref[:, 4 * PAIR :]


def pair_up(keys, values):
    return pl.pallas_call(
        pair_kernel,
        out_shape=(
            jax.ShapeDtypeStruct((ROWS, KVH * PAIR), jnp.bfloat16),
            jax.ShapeDtypeStruct((ROWS, 4 * PAIR), jnp.bfloat16),
        ),
    )(keys, values)


def on_device(query_rows, key_rows, value_rows, lengths):
    grp = lax.axis_index("grp")
    hd = lax.axis_index("hd")
    core, y, x_lo = grp % 2, (grp // 2) % 4, grp // 8
    z, x_hi = hd % 4, hd // 4
    query = query_rows[0]
    kv, top = pair_up(key_rows[0], value_rows[0])

    def on_hd(value, pairs):
        return lax.ppermute(value, "hd", pairs)

    def on_grp(value, pairs):
        return lax.ppermute(value, "grp", pairs)

    def along_y(value, d):
        return on_grp(value, [(g, (g & 9) | ((g + 2 * d) & 6)) for g in range(16)])

    def along_z(value, d):
        return on_hd(value, [(4 * x + i, 4 * x + (i + d) % 4) for x in range(2) for i in range(4)])

    def swap(value):
        return on_grp(value, [(g, g ^ 1) for g in range(16)])

    def along_x_hi(value):
        return on_hd(value, [(i, i ^ 4) for i in range(8)])

    tie = lax.optimization_barrier

    steps = (0, 1, 3, 2)
    heads = [4 * c + (y - d) % 4 for c in (core, 1 - core) for d in steps]
    pre_len = jnp.where(grp == 0, 0, lengths[0])
    n_live = lengths[grp] - hd * ROWS
    info = jnp.stack([jnp.int32(v) for v in heads + [x_hi, z, pre_len, n_live]])

    r0x, r0p, r0m = along_x_hi(kv), along_z(kv, 1), along_z(kv, 3)
    four = jnp.where(core == 0, kv[:, : 4 * PAIR], swap(top))
    one = four[:, :PAIR]
    for d in range(1, 4):
        one = jnp.where(y == d, along_y(four[:, d * PAIR : (d + 1) * PAIR], d), one)
    r0x, r0p, r0m, one = tie((r0x, r0p, r0m, one))

    piece = jnp.where(x_lo == 0, one, on_grp(one, [(g, g ^ 8) for g in range(16)]))
    other, r0x_t, r0m_t = tie((along_x_hi(piece), r0x, r0m))
    both = jnp.stack(
        [jnp.where(x_hi == 0, piece, other), jnp.where(x_hi == 0, other, piece)]
    )

    r1x, r1p, r1m = along_x_hi(r0m_t), along_z(r0x_t, 1), along_z(r0m_t, 3)
    r2a, r2b = along_x_hi(r1m[: ROWS // 2]), along_z(r1p[ROWS // 2 :], 1)
    behind = [both] + [along_z(both, d) for d in range(1, 4)]
    orders = [
        jnp.stack([behind[(at - i) % 4] for i in range(4)], 1).reshape(8 * ROWS, PAIR)
        for at in range(4)
    ]
    mine = lax.select_n(z, *orders)
    position = lax.broadcasted_iota(jnp.int32, mine.shape, 0)
    lane = lax.broadcasted_iota(jnp.int32, mine.shape, 1)
    mine = jnp.where((lane < DH) | (position < lengths[0]), mine, 0)

    parts = [mine] + [along_y(mine, d) for d in steps[1:]]
    own = (kv, r0p, r0m, r1m, r0x, r1x, r1p, r2a, r2b)
    state = attend_own(info, query, own)
    parts, state = tie((parts, state))
    swapped = [swap(value) for value in parts]
    out = attend_prompt(info, query, state, parts, own, 0, None)
    return attend_prompt(info, query, state, swapped, own, 4, out)[None]


def solution(mesh):
    placed = (P("grp", "hd", None), P("grp", "hd", None), P("grp", "hd", None), P())
    return jax.shard_map(
        on_device, mesh=mesh, in_specs=placed, out_specs=P("grp", "hd", None), check_vma=False
    )
```

```python
import functools
import math

import jax
import jax.numpy as jnp
from jax import lax
from jax.experimental import pallas as pl
from jax.experimental.pallas import tpu as pltpu
from jax.sharding import PartitionSpec as P

DH = 128
ROWS = 128
KVH = 8
GROUP = 8
PAIR = 2 * DH
SCALE_LOG2 = math.log2(math.e) / math.sqrt(DH)
NEG = -1e30
LEAST, MOST = 2.0**-80, 2.0**100
NT = (((1,), (1,)), ((), ()))
TILE = 256
IN_TILE = TILE // ROWS
PARAMS = pltpu.CompilerParams(vmem_limit_bytes=24 << 20)


def cost(heads, keys):
    pairs = GROUP * heads * ROWS * keys
    return pl.CostEstimate(flops=8 * pairs * DH, bytes_accessed=1 << 22, transcendentals=pairs)


def tiles(q_ref, head):
    for t in range(GROUP // IN_TILE):
        lanes = [lane_of(head, h) for h in range(t * IN_TILE, (t + 1) * IN_TILE)]
        yield t, jnp.concatenate([q_ref[:, lane] for lane in lanes], 0)


def lane_of(head, h):
    return pl.ds(pl.multiple_of((head * GROUP + h) * DH, DH), DH)


def causal_mask():
    row = lax.broadcasted_iota(jnp.int32, (TILE, ROWS), 0) % ROWS
    return row >= lax.broadcasted_iota(jnp.int32, (TILE, ROWS), 1)


def sweep(q_ref, head, k_scr, v_scr, n_keys, causal, put):
    for t, q in tiles(q_ref, head):
        s = lax.dot_general(q, k_scr[:n_keys, :], NT, preferred_element_type=jnp.float32)
        s = s * SCALE_LOG2
        if causal:
            s = jnp.concatenate([jnp.where(causal_mask(), s[:, :ROWS], NEG), s[:, ROWS:]], 1)
        p = jnp.exp2(s).astype(jnp.bfloat16)
        sums = jnp.dot(p, v_scr[:n_keys, :], preferred_element_type=jnp.float32)
        for j in range(IN_TILE):
            put(t * IN_TILE + j, sums[j * ROWS : (j + 1) * ROWS])


def place(k_scr, v_scr, slot, ref, ok):
    rows = slice(slot * ROWS, (slot + 1) * ROWS)
    k_scr[rows, :] = ref[:, :DH]
    v_scr[rows, :DH] = jnp.where(ok, ref[:, DH:], jnp.zeros_like(ref[:, DH:]))
    v_scr[rows, DH:] = jnp.where(ok, jnp.ones((ROWS, DH), jnp.float32), 0.0).astype(jnp.bfloat16)


def own_blocks(info):
    z, right = info[9], info[8] == 1
    return (True, z >= 1, z == 3, z >= 2, right, right, right, right)


def own_kernel(info, q_ref, *rest):
    blocks, (tot_ref, acc_ref, k_own, v_own) = rest[:9], rest[9:]
    head = pl.program_id(0)
    allowed = own_blocks(info)
    columns = pl.ds(pl.multiple_of(head * PAIR, PAIR), PAIR)
    half = pl.ds(pl.multiple_of(lax.rem(head, 4) * PAIR, PAIR), PAIR)

    @pl.when(info[11] > 0)
    def _():
        for slot in range(4):
            place(k_own, v_own, slot, blocks[slot][:, columns], allowed[slot])

        for slot in range(4, 7):
            place(k_own, v_own, slot, blocks[slot][:, columns], allowed[slot])

        @pl.when(head < 4)
        def _():
            place(k_own, v_own, 7, blocks[7][:, half], allowed[7])

        @pl.when(head >= 4)
        def _():
            place(k_own, v_own, 7, blocks[8][:, half], allowed[7])

        lane = lax.broadcasted_iota(jnp.int32, (ROWS, DH), 1)

        def run(n_keys):
            totals = []

            def put(h, sums):
                acc_ref[:, lane_of(head, h)] = sums[:, :DH]
                totals.append(jnp.where(lane == h, sums[:, DH:], totals[-1] if totals else 0.0))

            sweep(q_ref, head, k_own, v_own, n_keys, True, put)
            tot_ref[:, pl.ds(pl.multiple_of(head * DH, DH), DH)] = totals[-1]

        @pl.when(info[8] == 1)
        def _():
            run(8 * ROWS)

        @pl.when(info[8] == 0)
        def _():
            run(4 * ROWS)


def prompt_kernel(first, count, aliased, info, q_ref, tot_in, acc_in, *rest):
    prompt, stored, rest = rest[:count], rest[count : count + 9], rest[count + 9 + aliased :]
    o_hbm, k_pre, v_pre, out, flags, sems = rest[:6]
    pre_len, n_live = info[10], info[11]
    chunks = (pre_len + 255) // 256
    row = lax.broadcasted_iota(jnp.int32, (ROWS, DH), 0)

    def store(i):
        columns = pl.ds(pl.multiple_of(info[first + i] * GROUP * DH, GROUP * DH), GROUP * DH)
        return pltpu.make_async_copy(out.at[i], o_hbm.at[:, columns], sems.at[i])

    def take(i):
        for n, buffer in enumerate(prompt):

            @pl.when(i == n)
            def _(buffer=buffer):
                k_pre[...] = buffer[:, :DH]
                v_pre[:, :DH] = buffer[:, DH:]

    def attend(n_keys):
        @pl.loop(0, count)
        def _(i):
            head = info[first + i]
            take(i)
            flags[i] = jnp.zeros((ROWS, DH), jnp.float32)

            def finish(h, sums):
                totals = tot_in[:, pl.ds(pl.multiple_of(head * DH, DH), DH)]
                total = totals[:, h : h + 1]
                value = acc_in[:, lane_of(head, h)]
                if sums is None:
                    total = jnp.broadcast_to(total, (ROWS, DH))
                else:
                    total = total + sums[:, DH:]
                    value = value + sums[:, :DH]
                wrong = jnp.where((total >= LEAST) & (total <= MOST), 0.0, 1.0)
                flags[i] = jnp.maximum(flags[i], jnp.where(row < n_live, wrong, 0.0))
                value = jnp.where(row < n_live, value / total, 0.0)
                out[i, :, h * DH : (h + 1) * DH] = value.astype(jnp.bfloat16)

            if n_keys == 0:
                for h in range(GROUP):
                    finish(h, None)
            else:
                sweep(q_ref, head, k_pre, v_pre, n_keys, False, finish)
            store(i).start()

    @pl.when(n_live > 0)
    def _():
        live = lax.broadcasted_iota(jnp.int32, (8 * ROWS, DH), 0) < pre_len
        v_pre[:, DH:] = jnp.where(live, 1.0, 0.0).astype(jnp.bfloat16)
        for n in (0, 2, 3, 4):

            @pl.when((chunks == n) | ((n == 2) & (chunks == 1)))
            def _(n=n):
                attend(256 * n)

    @pl.when(n_live <= 0)
    def _():
        out[...] = jnp.zeros_like(out)
        for i in range(count):
            store(i).start()

    for i in range(count):
        store(i).wait()

    @pl.when(n_live > 0)
    def _():
        @pl.when(jnp.max(flags[...]) > 0.5)
        def _():
            @pl.loop(0, count)
            def _(i):
                @pl.when(jnp.max(flags[i]) > 0.5)
                def _():
                    take(i)
                    with_largest(
                        info, info[first + i], q_ref, k_pre, v_pre, stored, out.at[i], *rest[6:]
                    )
                    store(i).start()
                    store(i).wait()


def with_largest(info, head, q_ref, k_pre, v_pre, stored, o_ref, k_aug, v_aug, land, sem):
    pre_len, n_live = info[10], info[11]
    allowed = own_blocks(info)

    def put(rows, count, key, value, ok):
        first = lax.broadcasted_iota(jnp.int32, (count, DH), 1) == 0
        k_aug[rows, :DH] = key
        k_aug[rows, DH:] = jnp.where(first & jnp.logical_not(ok), NEG, 0.0).astype(jnp.bfloat16)
        v_aug[rows, :DH] = value
        v_aug[rows, DH:] = jnp.ones((count, DH), jnp.bfloat16)

    def fetch(source, columns):
        copy = pltpu.make_async_copy(source.at[:, columns], land, sem)
        copy.start()
        copy.wait()

    columns = pl.ds(pl.multiple_of(head * PAIR, PAIR), PAIR)
    half = pl.ds(pl.multiple_of(lax.rem(head, 4) * PAIR, PAIR), PAIR)
    for slot in range(8):
        if slot < 7:
            fetch(stored[slot], columns)
        else:
            for low, source in ((True, stored[7]), (False, stored[8])):

                @pl.when((head < 4) == low)
                def _(source=source):
                    fetch(source, half)

        rows = slice(slot * ROWS, (slot + 1) * ROWS)
        put(rows, ROWS, land[:, :DH], land[:, DH:], allowed[slot])
    position = lax.broadcasted_iota(jnp.int32, (8 * ROWS, DH), 0)
    rows = slice(8 * ROWS, 16 * ROWS)
    put(rows, 8 * ROWS, k_pre[...], v_pre[:, :DH], position < pre_len)

    row = lax.broadcasted_iota(jnp.int32, (ROWS, PAIR), 0)
    col = lax.broadcasted_iota(jnp.int32, (ROWS, PAIR), 1)
    one = jnp.where(col[:, :DH] == 0, 1.0, 0.0).astype(jnp.bfloat16)

    @pl.loop(0, GROUP)
    def _(h):
        lane = pl.ds(pl.multiple_of(h * DH, DH), DH)
        q = jnp.concatenate([q_ref[:, lane_of(head, h)], one], 1)

        def scores(c):
            keys = pl.ds(pl.multiple_of(c * PAIR, PAIR), PAIR)
            s = lax.dot_general(q, k_aug[keys, :], NT, preferred_element_type=jnp.float32)
            return jnp.where((row >= col) | (col >= ROWS) | (c > 0), s, NEG), keys

        def largest(c, top):
            return jnp.maximum(top, jnp.max(scores(c)[0], axis=1, keepdims=True))

        top = lax.fori_loop(0, 8, largest, jnp.full((ROWS, 1), NEG, jnp.float32))

        def weigh(c, acc):
            s, keys = scores(c)
            p = jnp.exp2((s - top) * SCALE_LOG2).astype(jnp.bfloat16)
            return acc + jnp.dot(p, v_aug[keys, :], preferred_element_type=jnp.float32)

        acc = lax.fori_loop(0, 8, weigh, jnp.zeros((ROWS, PAIR), jnp.float32))
        out = jnp.where(row[:, :DH] < n_live, acc[:, :DH] / acc[:, DH:], 0.0)
        o_ref[:, lane] = out.astype(jnp.bfloat16)


VMEM = pl.BlockSpec(memory_space=pltpu.VMEM)
ANY = pl.BlockSpec(memory_space=pl.ANY)


def scratch():
    return [
        pltpu.VMEM((8 * ROWS, DH), jnp.bfloat16),
        pltpu.VMEM((8 * ROWS, PAIR), jnp.bfloat16),
    ]


def attend_own(info, query, own):
    return pl.pallas_call(
        own_kernel,
        grid_spec=pltpu.PrefetchScalarGridSpec(
            num_scalar_prefetch=1,
            grid=(KVH,),
            in_specs=[VMEM] * (1 + len(own)),
            out_specs=(VMEM, VMEM),
            scratch_shapes=scratch(),
        ),
        out_shape=(
            jax.ShapeDtypeStruct((ROWS, KVH * DH), jnp.float32),
            jax.ShapeDtypeStruct((ROWS, KVH * GROUP * DH), jnp.float32),
        ),
        compiler_params=PARAMS,
        cost_estimate=cost(KVH, 8 * ROWS),
        name="own",
    )(info, query, *own)


def attend_prompt(info, query, state, prompt, own, first, before):
    last = () if before is None else (before,)
    operands = (info, query, *state, *prompt, *own, *last)
    count = len(prompt)
    return pl.pallas_call(
        functools.partial(prompt_kernel, first, count, len(last)),
        grid_spec=pltpu.PrefetchScalarGridSpec(
            num_scalar_prefetch=1,
            grid=(1,),
            in_specs=[VMEM] * (3 + count) + [ANY] * (len(own) + len(last)),
            out_specs=ANY,
            scratch_shapes=scratch()
            + [
                pltpu.VMEM((count, ROWS, GROUP * DH), jnp.bfloat16),
                pltpu.VMEM((count, ROWS, DH), jnp.float32),
                pltpu.SemaphoreType.DMA((count,)),
                pltpu.VMEM((16 * ROWS, PAIR), jnp.bfloat16),
                pltpu.VMEM((16 * ROWS, PAIR), jnp.bfloat16),
                pltpu.VMEM((ROWS, PAIR), jnp.bfloat16),
                pltpu.SemaphoreType.DMA(()),
            ],
        ),
        out_shape=jax.ShapeDtypeStruct(query.shape, jnp.bfloat16),
        input_output_aliases={} if before is None else {len(operands) - 1: 0},
        compiler_params=PARAMS,
        cost_estimate=cost(count, 8 * ROWS),
        name=f"prompt{first}",
    )(*operands)


def pair_kernel(k_ref, v_ref, o_ref, top_ref):
    for h in range(KVH):
        o_ref[:, h * PAIR : h * PAIR + DH] = k_ref[:, h * DH : (h + 1) * DH]
        o_ref[:, h * PAIR + DH : (h + 1) * PAIR] = v_ref[:, h * DH : (h + 1) * DH]
    top_ref[...] = o_ref[:, 4 * PAIR :]


def pair_up(keys, values):
    return pl.pallas_call(
        pair_kernel,
        out_shape=(
            jax.ShapeDtypeStruct((ROWS, KVH * PAIR), jnp.bfloat16),
            jax.ShapeDtypeStruct((ROWS, 4 * PAIR), jnp.bfloat16),
        ),
    )(keys, values)


def on_device(query_rows, key_rows, value_rows, lengths):
    grp = lax.axis_index("grp")
    hd = lax.axis_index("hd")
    core, y, x_lo = grp % 2, (grp // 2) % 4, grp // 8
    z, x_hi = hd % 4, hd // 4
    query = query_rows[0]
    kv, top = pair_up(key_rows[0], value_rows[0])

    def on_hd(value, pairs):
        return lax.ppermute(value, "hd", pairs)

    def on_grp(value, pairs):
        return lax.ppermute(value, "grp", pairs)

    def along_y(value, d):
        return on_grp(value, [(g, (g & 9) | ((g + 2 * d) & 6)) for g in range(16)])

    def along_z(value, d):
        return on_hd(value, [(4 * x + i, 4 * x + (i + d) % 4) for x in range(2) for i in range(4)])

    def swap(value):
        return on_grp(value, [(g, g ^ 1) for g in range(16)])

    def along_x_hi(value):
        return on_hd(value, [(i, i ^ 4) for i in range(8)])

    tie = lax.optimization_barrier

    steps = (0, 1, 3, 2)
    heads = [4 * c + (y - d) % 4 for c in (core, 1 - core) for d in steps]
    pre_len = jnp.where(grp == 0, 0, lengths[0])
    n_live = lengths[grp] - hd * ROWS
    info = jnp.stack([jnp.int32(v) for v in heads + [x_hi, z, pre_len, n_live]])

    r0x, r0p, r0m = along_x_hi(kv), along_z(kv, 1), along_z(kv, 3)
    four = jnp.where(core == 0, kv[:, : 4 * PAIR], swap(top))
    one = four[:, :PAIR]
    for d in range(1, 4):
        one = jnp.where(y == d, along_y(four[:, d * PAIR : (d + 1) * PAIR], d), one)
    r0x, r0p, r0m, one = tie((r0x, r0p, r0m, one))

    piece = jnp.where(x_lo == 0, one, on_grp(one, [(g, g ^ 8) for g in range(16)]))
    other, r0m_t = tie((along_x_hi(piece), r0m))
    both = jnp.stack(
        [jnp.where(x_hi == 0, piece, other), jnp.where(x_hi == 0, other, piece)]
    )

    r1x, r1p, r1m = along_x_hi(r0m_t), along_z(r0x, 1), along_z(r0m, 3)
    r2a, r2b = along_x_hi(r1m[:, : 4 * PAIR]), along_z(r1p[:, 4 * PAIR :], 1)
    behind = [both] + [along_z(both, d) for d in range(1, 4)]
    orders = [
        jnp.stack([behind[(at - i) % 4] for i in range(4)], 1).reshape(8 * ROWS, PAIR)
        for at in range(4)
    ]
    mine = lax.select_n(z, *orders)
    position = lax.broadcasted_iota(jnp.int32, mine.shape, 0)
    lane = lax.broadcasted_iota(jnp.int32, mine.shape, 1)
    mine = jnp.where((lane < DH) | (position < lengths[0]), mine, 0)

    parts = [mine] + [along_y(mine, d) for d in steps[1:]]
    own = (kv, r0p, r0m, r1m, r0x, r1x, r1p, r2a, r2b)
    state = attend_own(info, query, own)
    parts, state = tie((parts, state))
    swapped = [swap(value) for value in parts]
    out = attend_prompt(info, query, state, parts, own, 0, None)
    return attend_prompt(info, query, state, swapped, own, 4, out)[None]


def solution(mesh):
    placed = (P("grp", "hd", None), P("grp", "hd", None), P("grp", "hd", None), P())
    return jax.shard_map(
        on_device, mesh=mesh, in_specs=placed, out_specs=P("grp", "hd", None), check_vma=False
    )
```
